1024 devices in a mesh: front: 16 (over z, core), row: 8 (over y), col: 8 (over x).
Axes of the slice: x: 8, y: 8, z: 8, core: 2. Of those that a mesh axis runs over, the one named last changes fastest.
Arguments:
- tile: float32 [16, 2048, 4096], P('front', 'row', 'col'), may hold values from -6 to 6
- top_block: float32 [16, 256, 4096], P('front', None, 'col'), may hold values from -6 to 6
- reflectors: float32 [16, 2048, 256], P('front', 'row'), may hold values from -0.375 to 0.375
- panel_t: float32 [16, 2048, 256], P('front', 'row'), as said below
- parent: int32 [16], replicated, may hold values from 0 to 65535
- send_rows: int32 [16, 8, 8, 32], P('front', 'row'), may hold values from 0 to 255, as said below
- send_count: int32 [16, 8, 8], P('front', 'row'), may hold values from 24 to 32, as said below
- parent_reflectors: float32 [16, 4096, 256], P('front', 'row'), may hold values from -0.25 to 0.25
- parent_t: float32 [16, 2048, 256], P('front', 'row'), as said below
Outputs:
- renewed_tile: float32 [16, 2048, 4096], P('front', 'row', 'col')
- top_after: float32 [16, 2048, 4096], P('front', 'row', 'col')
- assembled: float32 [16, 4096, 4096], P('front', 'row', 'col')
The draws below stay inside these ranges and needn't reach their ends.
Inputs may be any that keep to these rules, and one draw needn't show every extreme that they name: `send_rows`: within one row owner of one front the listed indices are distinct rows of its 256 rows. `send_count`: each row owner of each front has a slot that sends exactly 32 rows. `panel_t`: upper triangular. `parent_t`: upper triangular.
All inputs are finite; a program needn't handle non-finite values.
Results may differ from the reference program's by a relative error of at most 0.0003.
Values sent between devices are 32-bit elements; how exact they have to be, the bound alone decides.
A program may use at most 64 MiB of HBM per device.

```python
import jax
import jax.numpy as jnp
from jax import lax

B = 256
ROWS_DEV = 256
CAP = 32
SPREAD = 8
ROWS = 2048
COLS = 4096
N_FRONT = 16
N_ROW = 8


def triangle(key, lowest, highest, spread):
    first, second = jax.random.split(key)
    shape = (N_FRONT, N_ROW, B, B)
    diagonal = jax.random.uniform(first, (N_FRONT, N_ROW, B), jnp.float32, lowest, highest)
    rough = jax.random.normal(second, shape, jnp.float32) * (spread / B ** 0.5)
    upper = jnp.arange(B)[None, :] > jnp.arange(B)[:, None]
    result = jnp.where(upper[None, None], rough, 0.0) + diagonal[..., None] * jnp.eye(B, dtype=jnp.float32)[None, None]
    return result.reshape(N_FRONT, N_ROW * B, B)


def draw_panel_t(key, part):
    key = jax.random.fold_in(key, 11)
    return triangle(key, 1.3, 1.97, 0.5)


def draw_parent_t(key, part):
    key = jax.random.fold_in(key, 23)
    return triangle(key, 1.1, 1.9, 0.5)


def draw_send_rows(key, part):
    key = jax.random.fold_in(key, 37)
    scores = jax.random.randint(key, (N_FRONT, N_ROW, ROWS_DEV), 0, 1 << 20) * ROWS_DEV
    scores = scores + jnp.arange(ROWS_DEV, dtype=jnp.int32)[None, None, :]
    order = jnp.argsort(scores, axis=2, stable=True).astype(jnp.int32)
    return order[:, :, :SPREAD * CAP].reshape(N_FRONT, N_ROW, SPREAD, CAP)


def draw_send_count(key, part):
    key = jax.random.fold_in(key, 41)
    first, second = jax.random.split(key)
    counts = jax.random.randint(first, (N_FRONT, N_ROW, SPREAD), CAP - CAP // 4, CAP + 1)
    fullest = jax.random.randint(second, (N_FRONT, N_ROW, 1), 0, SPREAD)
    slots = jnp.arange(SPREAD, dtype=jnp.int32)[None, None, :]
    return jnp.where(slots == fullest, CAP, counts).astype(jnp.int32)


def plant(entries, key, smallest, high):
    shape = entries.shape
    index_at = [jax.random.randint(jax.random.fold_in(key, axis), (), 0, shape[axis]) for axis in range(len(shape))]
    entries = entries.at[tuple(index_at)].set(smallest)
    longest = shape.index(max(shape))
    index_at[longest] = (index_at[longest] + 1) % shape[longest]
    return entries.at[tuple(index_at)].set(high)


def block_scale(rng, extent, cuts, low, largest):
    factor_of, own = 1.0, jax.random.fold_in(rng, 6)
    for position, parts in cuts:
        steps = jnp.exp(jax.random.uniform(jax.random.fold_in(own, position), (parts,), jnp.float32, low / len(cuts), largest / len(cuts)))
        factor_of = factor_of * jnp.repeat(steps, extent[position] // parts).reshape([-1 if axis == position else 1 for axis in range(len(extent))])
    return factor_of


def noise(stream_key, shape, scale, bound, cuts=(), held_as=jnp.bfloat16):
    loudness = block_scale(stream_key, shape, cuts, -0.22, 0.18) if cuts else 1.0
    entries = jax.random.normal(stream_key, shape, jnp.float32) * scale * loudness
    return jnp.minimum(jnp.maximum(entries, -bound), bound).astype(held_as)


def setup_inputs(seed: int = 0) -> dict:
    arg_keys = jax.random.split(jax.random.key(seed), 10)
    tile = noise(arg_keys[0], (N_FRONT, ROWS, COLS), 1.0, 6.0, ((0, 16), (1, 8), (2, 8)), jnp.float32)
    top_block = noise(arg_keys[1], (N_FRONT, B, COLS), 1.0, 6.0, ((0, 16), (2, 8)), jnp.float32)
    reflectors = noise(arg_keys[2], (N_FRONT, ROWS, B), ROWS_DEV ** -0.5, 0.375, ((0, 16), (1, 8)), jnp.float32)
    panel_t = draw_panel_t(jax.random.fold_in(arg_keys[9], 71), 0)
    parent = plant(jax.random.randint(arg_keys[4], (N_FRONT,), 0, 4096 * N_FRONT), jax.random.fold_in(arg_keys[4], 1), 0, (4096 * N_FRONT) - 1).astype(jnp.int32)
    send_rows = draw_send_rows(jax.random.fold_in(arg_keys[9], 71), 0)
    send_count = draw_send_count(jax.random.fold_in(arg_keys[9], 71), 0)
    parent_reflectors = noise(arg_keys[7], (N_FRONT, N_ROW * N_FRONT * CAP, B), (N_FRONT * CAP) ** -0.5, 0.25, ((0, 16), (1, 8)), jnp.float32)
    parent_t = draw_parent_t(jax.random.fold_in(arg_keys[9], 71), 0)
    return {"tile": tile, "top_block": top_block, "reflectors": reflectors, "panel_t": panel_t, "parent": parent, "send_rows": send_rows, "send_count": send_count, "parent_reflectors": parent_reflectors, "parent_t": parent_t}


PRECISION = lax.Precision.HIGHEST


def product(left, right):
    return jnp.dot(left, right, precision=PRECISION, preferred_element_type=jnp.float32)


def transposed(left, right):
    return lax.dot_general(left, right, (((0,), (0,)), ((), ())), precision=PRECISION, preferred_element_type=jnp.float32)


def reference(tile, top_block, reflectors, panel_t, parent, send_rows, send_count, parent_reflectors, parent_t):
    columns = tile.shape[2]

    def one_front(pieces):
        front_tile, initial, front_vectors, front_factor = pieces
        blocks = front_tile.reshape(N_ROW, ROWS_DEV, columns)
        vectors = front_vectors.reshape(N_ROW, ROWS_DEV, B)
        factors = front_factor.reshape(N_ROW, B, B)
        current = initial
        renewed_list = []
        leaving_list = []
        for owner in range(N_ROW):
            projected = transposed(vectors[owner], blocks[owner])
            update = transposed(factors[owner], current + projected)
            renewed_list.append(blocks[owner] - product(vectors[owner], update))
            current = current - update
            leaving_list.append(current)
        return jnp.stack(renewed_list), jnp.concatenate(leaving_list, 0)

    renewed, leaving = lax.map(one_front, (tile, top_block, reflectors, panel_t))
    occupied = jnp.arange(CAP, dtype=jnp.int32)[None, None, None, :] < send_count[..., None]

    def one_group(pieces):
        group, group_vectors, group_factor = pieces
        offsets = jnp.mod(group - parent, N_FRONT).astype(jnp.int32)
        usable = offsets < SPREAD
        clipped = jnp.minimum(offsets, SPREAD - 1).astype(jnp.int32)
        indices = jnp.take_along_axis(send_rows, clipped[:, None, None, None], axis=2)[:, :, 0]
        keeping = jnp.take_along_axis(occupied, clipped[:, None, None, None], axis=2)[:, :, 0]
        keeping = jnp.logical_and(keeping, usable[:, None, None])
        rows = jnp.take_along_axis(renewed, indices[..., None], axis=2)
        rows = jnp.where(keeping[..., None], rows, jnp.zeros_like(rows))
        stacked = rows.transpose(1, 0, 2, 3).reshape(N_ROW, N_FRONT * CAP, columns)
        vectors = group_vectors.reshape(N_ROW, N_FRONT * CAP, B)
        factors = group_factor.reshape(N_ROW, B, B)
        inner_sums = jnp.einsum("orb,orc->obc", vectors, stacked, precision=PRECISION)
        weights = jnp.einsum("oab,oac->obc", factors, inner_sums, precision=PRECISION)
        result = stacked - jnp.einsum("orb,obc->orc", vectors, weights, precision=PRECISION)
        return result.reshape(N_ROW * N_FRONT * CAP, columns)

    assembled = lax.map(one_group, (jnp.arange(N_FRONT, dtype=jnp.int32), parent_reflectors, parent_t))
    return renewed.reshape(N_FRONT, N_ROW * ROWS_DEV, columns), leaving, assembled
```

```python
import functools

import jax
import jax.numpy as jnp
from jax import lax
from jax.experimental import pallas as pl
from jax.experimental.pallas import tpu as pltpu
from jax.sharding import PartitionSpec as P

MESH = pl.DeviceIdType.MESH
F32, BF16 = jnp.float32, jnp.bfloat16
CHUNK = 128
PIECES = 4


def split(x):
    high = x.astype(BF16)
    return high, (x - high.astype(F32)).astype(BF16)


def dot(left, right):
    return jnp.dot(left, right, preferred_element_type=F32)


def left_triple(x):
    high, low = split(x)
    return jnp.concatenate([high, high, low], axis=1)


def right_triple(x):
    high, low = split(x)
    return jnp.concatenate([high, low, high], axis=0)


def kernel(
    n_front,
    n_row,
    tile_in,
    top_in,
    vectors_in,
    factor_in,
    rows_in,
    pvectors_in,
    pfactor_in,
    parent,
    count,
    renewed,
    after,
    assembled,
    tile,
    top,
    vectors,
    factor,
    rows_ref,
    pvectors,
    pfactor,
    loaded,
    vt3,
    v3,
    tth,
    ttl,
    pt3,
    p3,
    st3,
    gv3,
    picks,
    ga,
    proj,
    uh,
    ul,
    upd,
    top_rx,
    z_tx,
    z_rx,
    chain_send,
    chain_recv,
    z_send,
    z_recv,
):
    front, row = lax.axis_index("front"), lax.axis_index("row")
    size, cols = tile.shape
    chunks = cols // CHUNK
    piece = size // PIECES
    spread, cap = rows_ref.shape
    slots = n_front * cap

    pairs = (
        (vectors_in, vectors),
        (tile_in, tile),
        (factor_in, factor),
        (top_in, top),
        (rows_in, rows_ref),
        (pvectors_in, pvectors),
        (pfactor_in, pfactor),
    )
    loads = [pltpu.make_async_copy(a, b, loaded.at[i]) for i, (a, b) in enumerate(pairs)]
    for load in loads:
        load.start()

    barrier = pltpu.get_barrier_semaphore()

    def greet(step, carry):
        peer = lax.rem(front + step, n_front)
        pl.semaphore_signal(barrier, inc=1, device_id={"front": peer}, device_id_type=MESH)
        return carry

    @pl.when(row > 0)
    def _():
        pl.semaphore_signal(barrier, inc=1, device_id={"row": row - 1}, device_id_type=MESH)

    lax.fori_loop(1, n_front, greet, 0)

    def columns(c):
        return pl.ds(pl.multiple_of(c * CHUNK, CHUNK), CHUNK)

    def project(c):
        proj[c] = dot(vt3[...], right_triple(tile[:, columns(c)]))

    def chain_copy(c, q):
        part = pl.ds(q * piece, piece)
        return pltpu.make_async_remote_copy(
            src_ref=after.at[part, columns(c)],
            dst_ref=top_rx.at[c, part],
            send_sem=chain_send.at[c, q],
            recv_sem=chain_recv.at[c, q],
            device_id={"row": lax.rem(row + 1, n_row)},
            device_id_type=MESH,
        )

    def chain(c):
        for q in range(PIECES):
            part = pl.ds(q * piece, piece)
            depth = min(size, -(-(q + 1) * piece // 128) * 128)

            @pl.when(row == 0)
            def _():
                top_rx[c, part] = top[part, columns(c)]

            @pl.when(row > 0)
            def _():
                chain_copy(c, q).wait_recv()

            entering = top_rx[c, part]
            high, low = split(entering + proj[c, part])
            uh[part], ul[part] = high, low
            update = (
                dot(tth[part, :depth], uh[:depth])
                + dot(tth[part, :depth], ul[:depth])
                + dot(ttl[part, :depth], uh[:depth])
            )
            after[part, columns(c)] = entering - update
            upd[part] = update

            @pl.when(row < n_row - 1)
            def _():
                chain_copy(c, q).start()

    def z_copy(c, target, source):
        return pltpu.make_async_remote_copy(
            src_ref=z_tx.at[c, target],
            dst_ref=z_rx.at[c, source],
            send_sem=z_send.at[c, target],
            recv_sem=z_recv.at[c, source],
            device_id={"front": target},
            device_id_type=MESH,
        )

    def contribute(c):
        weights = right_triple(upd[...])
        z_tx[c] = (ga[c] - dot(gv3[...], weights)).reshape(n_front, cap, CHUNK)

        def send(step, carry):
            z_copy(c, lax.rem(front + step, n_front), front).start()
            return carry

        lax.fori_loop(1, n_front, send, 0)
        z_rx[c, front] = z_tx[c, front]
        renewed[:, columns(c)] = tile[:, columns(c)] - dot(v3[...], weights)

    loads[0].wait()
    vt3[...] = left_triple(vectors[...].T)
    loads[2].wait()
    high, low = split(factor[...].T)
    tth[...], ttl[...] = high, low
    uh[...] = jnp.zeros_like(uh)
    ul[...] = jnp.zeros_like(ul)
    loads[1].wait()
    project(0)
    loads[3].wait()

    pl.semaphore_wait(barrier, n_front - 1 + jnp.where(row < n_row - 1, 1, 0))

    @pl.when(row == 0)
    def _():
        chain(0)

    for load in loads[4:]:
        load.wait()

    first = lax.rem(parent[front], n_front)
    lane = lax.broadcasted_iota(jnp.int32, (1, cap), 1)
    listed = []
    for g in range(n_front):
        k = lax.rem(g + n_front - first, n_front)
        held = jnp.minimum(k, spread - 1)
        sent = jnp.where(k < spread, count[held], 0)
        listed.append(jnp.where(lane < sent, rows_ref[pl.ds(held, 1), :], -1))
    wanted = jnp.concatenate(listed, axis=1)
    chosen = lax.broadcasted_iota(jnp.int32, (size, slots), 0) == wanted
    picks[...] = jnp.where(chosen, 1.0, 0.0).T.astype(BF16)

    vh, vl = split(vectors[...])
    v3[...] = jnp.concatenate([vh, vh, vl], axis=1)
    gvh = dot(picks[...], vh).astype(BF16)
    gv3[...] = jnp.concatenate([gvh, gvh, dot(picks[...], vl).astype(BF16)], axis=1)

    def prepare(c, carry):
        th, tl = split(tile[:, columns(c)])
        ga[c] = dot(picks[...], th) + dot(picks[...], tl)

        @pl.when(c > 0)
        def _():
            project(c)

        return carry

    lax.fori_loop(0, chunks, prepare, 0)
    p3[...] = left_triple(pvectors[...])
    pt3[...] = left_triple(pvectors[...].T)
    st3[...] = left_triple(pfactor[...].T)

    def forward(c, carry):
        @pl.when(jnp.logical_or(row > 0, c > 0))
        def _():
            chain(c)

        contribute(c)
        return carry

    lax.fori_loop(0, chunks, forward, 0)

    def assemble(c, carry):
        def arrive(step, inner):
            z_copy(c, front, lax.rem(front + step, n_front)).wait_recv()
            return inner

        lax.fori_loop(1, n_front, arrive, 0)
        stacked = z_rx[c].reshape(slots, CHUNK)
        inner_sums = dot(pt3[...], right_triple(stacked))
        weights = dot(st3[...], right_triple(inner_sums))
        assembled[:, columns(c)] = stacked - dot(p3[...], right_triple(weights))
        return carry

    lax.fori_loop(0, chunks, assemble, 0)

    def finish(c, carry):
        def left(step, inner):
            z_copy(c, lax.rem(front + step, n_front), front).wait_send()
            return inner

        lax.fori_loop(1, n_front, left, 0)

        @pl.when(row < n_row - 1)
        def _():
            for q in range(PIECES):
                chain_copy(c, q).wait_send()

        return carry

    lax.fori_loop(0, chunks, finish, 0)


def solution(mesh):
    n_front, n_row = mesh.shape["front"], mesh.shape["row"]

    def shards(tile, top, vectors, factor, parent, rows, count, pvectors, pfactor):
        size, cols = tile.shape[1:]
        stacked = pvectors.shape[1]
        cap = rows.shape[3]
        chunks = cols // CHUNK
        vmem = pl.BlockSpec(memory_space=pltpu.VMEM)
        smem = pl.BlockSpec(memory_space=pltpu.SMEM)
        hbm = pl.BlockSpec(memory_space=pltpu.HBM)
        outs = pl.pallas_call(
            functools.partial(kernel, n_front, n_row),
            out_shape=(
                jax.ShapeDtypeStruct((size, cols), F32),
                jax.ShapeDtypeStruct((size, cols), F32),
                jax.ShapeDtypeStruct((stacked, cols), F32),
            ),
            in_specs=[hbm] * 7 + [smem] * 2,
            out_specs=(vmem, vmem, vmem),
            scratch_shapes=[
                pltpu.VMEM((size, cols), F32),
                pltpu.VMEM((size, cols), F32),
                pltpu.VMEM((size, size), F32),
                pltpu.VMEM((size, size), F32),
                pltpu.VMEM(rows.shape[2:], jnp.int32),
                pltpu.VMEM((stacked, size), F32),
                pltpu.VMEM((size, size), F32),
                pltpu.SemaphoreType.DMA((7,)),
                pltpu.VMEM((size, 3 * size), BF16),
                pltpu.VMEM((size, 3 * size), BF16),
                pltpu.VMEM((size, size), BF16),
                pltpu.VMEM((size, size), BF16),
                pltpu.VMEM((size, 3 * stacked), BF16),
                pltpu.VMEM((stacked, 3 * size), BF16),
                pltpu.VMEM((size, 3 * size), BF16),
                pltpu.VMEM((stacked, 3 * size), BF16),
                pltpu.VMEM((stacked, size), BF16),
                pltpu.VMEM((chunks, stacked, CHUNK), F32),
                pltpu.VMEM((chunks, size, CHUNK), F32),
                pltpu.VMEM((size, CHUNK), BF16),
                pltpu.VMEM((size, CHUNK), BF16),
                pltpu.VMEM((size, CHUNK), F32),
                pltpu.VMEM((chunks, size, CHUNK), F32),
                pltpu.VMEM((chunks, n_front, cap, CHUNK), F32),
                pltpu.VMEM((chunks, n_front, cap, CHUNK), F32),
                pltpu.SemaphoreType.DMA((chunks, PIECES)),
                pltpu.SemaphoreType.DMA((chunks, PIECES)),
                pltpu.SemaphoreType.DMA((chunks, n_front)),
                pltpu.SemaphoreType.DMA((chunks, n_front)),
            ],
            compiler_params=pltpu.CompilerParams(
                collective_id=0, has_side_effects=True, vmem_limit_bytes=60 * 1024 * 1024
            ),
        )(tile[0], top[0], vectors[0], factor[0], rows[0, 0], pvectors[0], pfactor[0], parent, count[0, 0])
        return tuple(out[None] for out in outs)

    placed = (
        P("front", "row", "col"),
        P("front", None, "col"),
        P("front", "row", None),
        P("front", "row", None),
        P(),
        P("front", "row", None, None),
        P("front", "row", None),
        P("front", "row", None),
        P("front", "row", None),
    )
    out = P("front", "row", "col")
    return jax.shard_map(
        shards, mesh=mesh, in_specs=placed, out_specs=(out, out, out), check_vma=False
    )
```

```python
import functools

import jax
import jax.numpy as jnp
from jax import lax
from jax.experimental import pallas as pl
from jax.experimental.pallas import tpu as pltpu
from jax.sharding import PartitionSpec as P

MESH = pl.DeviceIdType.MESH
F32, BF16 = jnp.float32, jnp.bfloat16
CHUNK = 128
PIECES = 8
WIDE = 256


def split(x):
    high = x.astype(BF16)
    return high, (x - high.astype(F32)).astype(BF16)


def dot(left, right):
    return jnp.dot(left, right, preferred_element_type=F32)


def by_rows(left, right):
    lh, ll = split(left)
    rh, rl = split(right)
    return lax.dot_general(
        jnp.concatenate([lh, lh, ll], axis=1),
        jnp.concatenate([rh, rl, rh], axis=1),
        (((1,), (1,)), ((), ())),
        preferred_element_type=F32,
    )


def left_triple(x):
    high, low = split(x)
    return jnp.concatenate([high, high, low], axis=1)


def right_triple(x):
    high, low = split(x)
    return jnp.concatenate([high, low, high], axis=0)


def kernel(
    n_front,
    n_row,
    tile_in,
    top_in,
    vectors_in,
    factor_in,
    rows_in,
    pvectors_in,
    pfactor_in,
    parent_in,
    count_in,
    renewed,
    after,
    assembled,
    tile,
    vectors,
    factor,
    rows_ref,
    pvectors,
    pfactor,
    parent,
    count,
    loaded,
    top_loaded,
    vt3,
    tth,
    ttl,
    vf3,
    gvf3,
    picks,
    ga,
    proj,
    u3,
    h3,
    top_rx,
    z_tx,
    z_rx,
    chain_send,
    chain_recv,
    z_send,
    z_recv,
):
    front, row = lax.axis_index("front"), lax.axis_index("row")
    size, cols = tile.shape
    chunks = cols // CHUNK
    piece = size // PIECES
    spread, cap = rows_ref.shape
    slots = n_front * cap

    def top_load(c):
        return pltpu.make_async_copy(
            top_in.at[:, pl.ds(c * CHUNK, CHUNK)], top_rx.at[c], top_loaded.at[c]
        )

    pairs = (
        (vectors_in, vectors),
        (tile_in, tile),
        (factor_in, factor),
        (rows_in, rows_ref),
        (parent_in, parent),
        (count_in, count),
        (pvectors_in, pvectors),
        (pfactor_in, pfactor),
    )
    loads = [pltpu.make_async_copy(a, b, loaded.at[i]) for i, (a, b) in enumerate(pairs)]
    for load in loads[:3]:
        load.start()

    @pl.when(row == 0)
    def _():
        for c in range(chunks):
            top_load(c).start()

    for load in loads[3:]:
        load.start()

    barrier = pltpu.get_barrier_semaphore()

    def greet(step, carry):
        peer = lax.rem(front + step, n_front)
        pl.semaphore_signal(barrier, inc=1, device_id={"front": peer}, device_id_type=MESH)
        return carry

    @pl.when(row > 0)
    def _():
        pl.semaphore_signal(barrier, inc=1, device_id={"row": row - 1}, device_id_type=MESH)

    lax.fori_loop(1, n_front, greet, 0)

    def columns(c):
        return pl.ds(pl.multiple_of(c * CHUNK, CHUNK), CHUNK)

    def chain_copy(c, q):
        part = pl.ds(q * piece, piece)
        return pltpu.make_async_remote_copy(
            src_ref=after.at[part, columns(c)],
            dst_ref=top_rx.at[c, part],
            send_sem=chain_send.at[c, q],
            recv_sem=chain_recv.at[c, q],
            device_id={"row": lax.rem(row + 1, n_row)},
            device_id_type=MESH,
        )

    def chain(c):
        for q in range(PIECES):
            part = pl.ds(q * piece, piece)
            depth = min(size, -(-(q + 1) * piece // 128) * 128)

            @pl.when(row > 0)
            def _():
                chain_copy(c, q).wait_recv()

            entering = top_rx[c, part]
            high, low = split(entering + proj[part, columns(c)])
            u3[part, columns(c)] = high
            u3[pl.ds(size + q * piece, piece), columns(c)] = low
            u3[pl.ds(2 * size + q * piece, piece), columns(c)] = high
            first = u3[:depth, columns(c)]
            update = (
                dot(tth[part, :depth], first)
                + dot(tth[part, :depth], u3[size : size + depth, columns(c)])
                + dot(ttl[part, :depth], first)
            )
            after[part, columns(c)] = entering - update

            @pl.when(row < n_row - 1)
            def _():
                chain_copy(c, q).start()

    def z_copy(c, target, source):
        return pltpu.make_async_remote_copy(
            src_ref=z_tx.at[c, target],
            dst_ref=z_rx.at[c, source],
            send_sem=z_send.at[c, target],
            recv_sem=z_recv.at[c, source],
            device_id={"front": target},
            device_id_type=MESH,
        )

    def contribute(c):
        outgoing = ga[:, columns(c)] - dot(gvf3[...], u3[:, columns(c)])
        z_tx[c] = outgoing.reshape(n_front, cap, CHUNK)

        def send(step, carry):
            z_copy(c, lax.rem(front + step, n_front), front).start()
            return carry

        lax.fori_loop(1, n_front, send, 0)
        z_rx[c, front] = z_tx[c, front]

    loads[0].wait()
    vt3[...] = left_triple(vectors[...].T)
    loads[2].wait()
    high, low = split(factor[...].T)
    tth[...], ttl[...] = high, low
    loads[1].wait()
    proj[...] = dot(vt3[...], right_triple(tile[...]))
    u3[...] = jnp.zeros_like(u3)

    pl.semaphore_wait(barrier, n_front - 1 + jnp.where(row < n_row - 1, 1, 0))

    @pl.when(row == 0)
    def _():
        for c in range(chunks):
            top_load(c).wait()
        chain(0)

    for load in loads[3:]:
        load.wait()

    first = lax.rem(parent[front], n_front)
    lane = lax.broadcasted_iota(jnp.int32, (1, cap), 1)
    listed = []
    for g in range(n_front):
        k = lax.rem(g + n_front - first, n_front)
        held = jnp.minimum(k, spread - 1)
        sent = jnp.where(k < spread, count[held], 0)
        listed.append(jnp.where(lane < sent, rows_ref[pl.ds(held, 1), :], -1))
    wanted = jnp.concatenate(listed, axis=1)
    chosen = lax.broadcasted_iota(jnp.int32, (size, slots), 0) == wanted
    picks[...] = jnp.where(chosen, 1.0, 0.0).T.astype(BF16)

    vh, vl = split(by_rows(vectors[...], factor[...]))
    vf3[...] = jnp.concatenate([vh, vh, vl], axis=1)
    gvh = dot(picks[...], vh).astype(BF16)
    gvf3[...] = jnp.concatenate([gvh, gvh, dot(picks[...], vl).astype(BF16)], axis=1)
    th, tl = split(tile[...])
    ga[...] = dot(picks[...], th) + dot(picks[...], tl)

    def forward(c, carry):
        @pl.when(jnp.logical_or(row > 0, c > 0))
        def _():
            chain(c)

        contribute(c)
        return carry

    lax.fori_loop(0, chunks, forward, 0)

    renewed[...] = tile[...] - dot(vf3[...], u3[...])
    h3[...] = left_triple(by_rows(by_rows(pvectors[...], pfactor[...]), pvectors[...]))

    for w in range(cols // WIDE):
        mine = range(w * WIDE // CHUNK, (w + 1) * WIDE // CHUNK)

        def arrive(step, inner):
            for c in mine:
                z_copy(c, front, lax.rem(front + step, n_front)).wait_recv()
            return inner

        lax.fori_loop(1, n_front, arrive, 0)
        stacked = jnp.concatenate([z_rx[c].reshape(slots, CHUNK) for c in mine], axis=1)
        assembled[:, w * WIDE : (w + 1) * WIDE] = stacked - dot(h3[...], right_triple(stacked))

    def finish(c, carry):
        def left(step, inner):
            z_copy(c, lax.rem(front + step, n_front), front).wait_send()
            return inner

        lax.fori_loop(1, n_front, left, 0)

        @pl.when(row < n_row - 1)
        def _():
            for q in range(PIECES):
                chain_copy(c, q).wait_send()

        return carry

    lax.fori_loop(0, chunks, finish, 0)


def write_out(*refs):
    results, arrays, sems = refs[:3], refs[3:6], refs[6]
    copies = [
        pltpu.make_async_copy(result, array, sems.at[i])
        for i, (result, array) in enumerate(zip(results, arrays))
    ]
    for copy in copies:
        copy.start()
    for copy in copies:
        copy.wait()


def solution(mesh):
    n_front, n_row = mesh.shape["front"], mesh.shape["row"]

    def shards(tile, top, vectors, factor, parent, rows, count, pvectors, pfactor):
        size, cols = tile.shape[1:]
        stacked = pvectors.shape[1]
        cap = rows.shape[3]
        chunks = cols // CHUNK
        vmem = pl.BlockSpec(memory_space=pltpu.VMEM)
        hbm = pl.BlockSpec(memory_space=pltpu.HBM)
        shapes = (
            jax.ShapeDtypeStruct((size, cols), F32),
            jax.ShapeDtypeStruct((size, cols), F32),
            jax.ShapeDtypeStruct((stacked, cols), F32),
        )
        operands = (
            tile[0], top[0], vectors[0], factor[0], rows[0, 0], pvectors[0], pfactor[0], parent, count[0, 0],
        )
        outs = pl.pallas_call(
            functools.partial(kernel, n_front, n_row),
            out_shape=shapes,
            in_specs=[hbm] * 9,
            out_specs=(vmem, vmem, vmem),
            scratch_shapes=[
                pltpu.VMEM((size, cols), F32),
                pltpu.VMEM((size, size), F32),
                pltpu.VMEM((size, size), F32),
                pltpu.VMEM(rows.shape[2:], jnp.int32),
                pltpu.VMEM((stacked, size), F32),
                pltpu.VMEM((size, size), F32),
                pltpu.SMEM(parent.shape, jnp.int32),
                pltpu.SMEM(count.shape[2:], jnp.int32),
                pltpu.SemaphoreType.DMA((8,)),
                pltpu.SemaphoreType.DMA((chunks,)),
                pltpu.VMEM((size, 3 * size), BF16),
                pltpu.VMEM((size, size), BF16),
                pltpu.VMEM((size, size), BF16),
                pltpu.VMEM((size, 3 * size), BF16),
                pltpu.VMEM((stacked, 3 * size), BF16),
                pltpu.VMEM((stacked, size), BF16),
                pltpu.VMEM((stacked, cols), F32),
                pltpu.VMEM((size, cols), F32),
                pltpu.VMEM((3 * size, cols), BF16),
                pltpu.VMEM((stacked, 3 * stacked), BF16),
                pltpu.VMEM((chunks, size, CHUNK), F32),
                pltpu.VMEM((chunks, n_front, cap, CHUNK), F32),
                pltpu.VMEM((chunks, n_front, cap, CHUNK), F32),
                pltpu.SemaphoreType.DMA((chunks, PIECES)),
                pltpu.SemaphoreType.DMA((chunks, PIECES)),
                pltpu.SemaphoreType.DMA((chunks, n_front)),
                pltpu.SemaphoreType.DMA((chunks, n_front)),
            ],
            compiler_params=pltpu.CompilerParams(
                collective_id=0, has_side_effects=True, vmem_limit_bytes=40 * 1024 * 1024
            ),
        )(*[pltpu.with_memory_space_constraint(operand, pltpu.HBM) for operand in operands])
        outs = pl.pallas_call(
            write_out,
            out_shape=shapes,
            in_specs=[vmem] * 3,
            out_specs=(hbm, hbm, hbm),
            scratch_shapes=[pltpu.SemaphoreType.DMA((3,))],
        )(*[pltpu.with_memory_space_constraint(o, pltpu.VMEM) for o in outs])
        return tuple(out[None] for out in outs)

    placed = (
        P("front", "row", "col"),
        P("front", None, "col"),
        P("front", "row", None),
        P("front", "row", None),
        P(),
        P("front", "row", None, None),
        P("front", "row", None),
        P("front", "row", None),
        P("front", "row", None),
    )
    out = P("front", "row", "col")
    return jax.shard_map(
        shards, mesh=mesh, in_specs=placed, out_specs=(out, out, out), check_vma=False
    )
```

```python
import functools

import jax
import jax.numpy as jnp
from jax import lax
from jax.experimental import pallas as pl
from jax.experimental.pallas import tpu as pltpu
from jax.sharding import PartitionSpec as P

MESH = pl.DeviceIdType.MESH
F32, BF16 = jnp.float32, jnp.bfloat16
CHUNK = 128
PIECES = 8
WIDE = 256
EARLY = 4


def split(x):
    high = x.astype(BF16)
    return high, (x - high.astype(F32)).astype(BF16)


def dot(left, right):
    return jnp.dot(left, right, preferred_element_type=F32)


def by_rows(left, right):
    lh, ll = split(left)
    rh, rl = split(right)
    return lax.dot_general(
        jnp.concatenate([lh, lh, ll], axis=1),
        jnp.concatenate([rh, rl, rh], axis=1),
        (((1,), (1,)), ((), ())),
        preferred_element_type=F32,
    )


def left_triple(x):
    high, low = split(x)
    return jnp.concatenate([high, high, low], axis=1)


def right_triple(x):
    high, low = split(x)
    return jnp.concatenate([high, low, high], axis=0)


def kernel(
    n_front,
    n_row,
    tile_in,
    top_in,
    vectors_in,
    factor_in,
    rows_in,
    pvectors_in,
    pfactor_in,
    parent_in,
    count_in,
    renewed,
    after,
    assembled,
    tile,
    vectors,
    factor,
    rows_ref,
    pvectors,
    pfactor,
    parent,
    count,
    loaded,
    top_loaded,
    vt3,
    tth,
    ttl,
    vf3,
    gvf3,
    picks,
    ga,
    proj,
    u3,
    h3,
    top_rx,
    z_tx,
    z_rx,
    chain_send,
    chain_recv,
    z_send,
    z_recv,
    fronts,
    everyone,
):
    front, row = lax.axis_index("front"), lax.axis_index("row")
    size, cols = tile.shape
    chunks = cols // CHUNK
    piece = size // PIECES
    spread, cap = rows_ref.shape
    slots = n_front * cap

    def top_load(c):
        return pltpu.make_async_copy(
            top_in.at[:, pl.ds(c * CHUNK, CHUNK)], top_rx.at[c], top_loaded.at[c]
        )

    pairs = (
        (vectors_in, vectors),
        (tile_in, tile),
        (factor_in, factor),
        (rows_in, rows_ref),
        (parent_in, parent),
        (count_in, count),
        (pvectors_in, pvectors),
        (pfactor_in, pfactor),
    )
    loads = [pltpu.make_async_copy(a, b, loaded.at[i]) for i, (a, b) in enumerate(pairs)]
    for load in loads[:3]:
        load.start()

    @pl.when(row == 0)
    def _():
        for c in range(chunks):
            top_load(c).start()

    for load in loads[3:]:
        load.start()

    barrier = pltpu.get_barrier_semaphore()
    last = n_row - 1

    def tell(sem, **device):
        pl.semaphore_signal(sem, inc=1, device_id=device, device_id_type=MESH)

    def tell_fronts(sem):
        def one(step, carry):
            tell(sem, front=lax.rem(front + step, n_front))
            return carry

        lax.fori_loop(1, n_front, one, 0)

    @pl.when(row > 0)
    def _():
        tell(barrier, row=row - 1)

    @pl.when(row < last)
    def _():
        tell(barrier, row=last)

    @pl.when(row == last)
    def _():
        tell_fronts(barrier)

    def columns(c):
        return pl.ds(pl.multiple_of(c * CHUNK, CHUNK), CHUNK)

    def chain_copy(c, q):
        part = pl.ds(q * piece, piece)
        return pltpu.make_async_remote_copy(
            src_ref=after.at[part, columns(c)],
            dst_ref=top_rx.at[c, part],
            send_sem=chain_send.at[c, q],
            recv_sem=chain_recv.at[c, q],
            device_id={"row": lax.rem(row + 1, n_row)},
            device_id_type=MESH,
        )

    def chain(c):
        for q in range(PIECES):
            part = pl.ds(q * piece, piece)
            depth = min(size, -(-(q + 1) * piece // 128) * 128)

            @pl.when(row > 0)
            def _():
                chain_copy(c, q).wait_recv()

            entering = top_rx[c, part]
            high, low = split(entering + proj[part, columns(c)])
            u3[part, columns(c)] = high
            u3[pl.ds(size + q * piece, piece), columns(c)] = low
            u3[pl.ds(2 * size + q * piece, piece), columns(c)] = high
            first = u3[:depth, columns(c)]
            update = (
                dot(tth[part, :depth], first)
                + dot(tth[part, :depth], u3[size : size + depth, columns(c)])
                + dot(ttl[part, :depth], first)
            )
            after[part, columns(c)] = entering - update

            @pl.when(row < n_row - 1)
            def _():
                chain_copy(c, q).start()

    def z_copy(c, target, source):
        return pltpu.make_async_remote_copy(
            src_ref=z_tx.at[c, target],
            dst_ref=z_rx.at[c, source],
            send_sem=z_send.at[c, target],
            recv_sem=z_recv.at[c, source],
            device_id={"front": target},
            device_id_type=MESH,
        )

    def contribute(c):
        outgoing = ga[:, columns(c)] - dot(gvf3[...], u3[:, columns(c)])
        z_tx[c] = outgoing.reshape(n_front, cap, CHUNK)

        def send(step, carry):
            z_copy(c, lax.rem(front + step, n_front), front).start()
            return carry

        lax.fori_loop(1, n_front, send, 0)
        z_rx[c, front] = z_tx[c, front]

    loads[0].wait()
    vt3[...] = left_triple(vectors[...].T)
    loads[2].wait()
    high, low = split(factor[...].T)
    tth[...], ttl[...] = high, low
    loads[1].wait()
    proj[...] = dot(vt3[...], right_triple(tile[...]))
    u3[...] = jnp.zeros_like(u3)

    @pl.when(row < last)
    def _():
        pl.semaphore_wait(barrier, 1)

    @pl.when(row == 0)
    def _():
        for c in range(chunks):
            top_load(c).wait()
        chain(0)

    for load in loads[3:]:
        load.wait()

    first = lax.rem(parent[front], n_front)
    lane = lax.broadcasted_iota(jnp.int32, (1, cap), 1)
    listed = []
    for g in range(n_front):
        k = lax.rem(g + n_front - first, n_front)
        held = jnp.minimum(k, spread - 1)
        sent = jnp.where(k < spread, count[held], 0)
        listed.append(jnp.where(lane < sent, rows_ref[pl.ds(held, 1), :], -1))
    wanted = jnp.concatenate(listed, axis=1)
    chosen = lax.broadcasted_iota(jnp.int32, (size, slots), 0) == wanted
    picks[...] = jnp.where(chosen, 1.0, 0.0).T.astype(BF16)

    vh, vl = split(by_rows(vectors[...], factor[...]))
    vf3[...] = jnp.concatenate([vh, vh, vl], axis=1)
    gvh = dot(picks[...], vh).astype(BF16)
    gvf3[...] = jnp.concatenate([gvh, gvh, dot(picks[...], vl).astype(BF16)], axis=1)
    th, tl = split(tile[...])
    ga[...] = dot(picks[...], th) + dot(picks[...], tl)

    @pl.when(row == last)
    def _():
        pl.semaphore_wait(barrier, n_front - 1 + last)
        tell_fronts(fronts)
        pl.semaphore_wait(fronts, n_front - 1)
        for r in range(last):
            tell(everyone, row=r)

    def walk(c):
        @pl.when(jnp.logical_or(row > 0, c > 0))
        def _():
            chain(c)

    @pl.when(row < EARLY)
    def _():
        def walk_on(c, carry):
            walk(c)
            return carry

        def give(c, carry):
            contribute(c)
            return carry

        lax.fori_loop(0, chunks, walk_on, 0)
        pl.semaphore_wait(everyone, 1)
        lax.fori_loop(0, chunks, give, 0)

    @pl.when(row >= EARLY)
    def _():
        def both(c, carry):
            walk(c)

            @pl.when(jnp.logical_and(row < last, c == 0))
            def _():
                pl.semaphore_wait(everyone, 1)

            contribute(c)
            return carry

        lax.fori_loop(0, chunks, both, 0)

    renewed[...] = tile[...] - dot(vf3[...], u3[...])
    h3[...] = left_triple(by_rows(by_rows(pvectors[...], pfactor[...]), pvectors[...]))

    for w in range(cols // WIDE):
        mine = range(w * WIDE // CHUNK, (w + 1) * WIDE // CHUNK)

        def arrive(step, inner):
            for c in mine:
                z_copy(c, front, lax.rem(front + step, n_front)).wait_recv()
            return inner

        lax.fori_loop(1, n_front, arrive, 0)
        stacked = jnp.concatenate([z_rx[c].reshape(slots, CHUNK) for c in mine], axis=1)
        assembled[:, w * WIDE : (w + 1) * WIDE] = stacked - dot(h3[...], right_triple(stacked))

    def finish(c, carry):
        def left(step, inner):
            z_copy(c, lax.rem(front + step, n_front), front).wait_send()
            return inner

        lax.fori_loop(1, n_front, left, 0)

        @pl.when(row < n_row - 1)
        def _():
            for q in range(PIECES):
                chain_copy(c, q).wait_send()

        return carry

    lax.fori_loop(0, chunks, finish, 0)


def write_out(*refs):
    results, arrays, sems = refs[:3], refs[3:6], refs[6]
    copies = [
        pltpu.make_async_copy(result, array, sems.at[i])
        for i, (result, array) in enumerate(zip(results, arrays))
    ]
    for copy in copies:
        copy.start()
    for copy in copies:
        copy.wait()


def solution(mesh):
    n_front, n_row = mesh.shape["front"], mesh.shape["row"]

    def shards(tile, top, vectors, factor, parent, rows, count, pvectors, pfactor):
        size, cols = tile.shape[1:]
        stacked = pvectors.shape[1]
        cap = rows.shape[3]
        chunks = cols // CHUNK
        vmem = pl.BlockSpec(memory_space=pltpu.VMEM)
        hbm = pl.BlockSpec(memory_space=pltpu.HBM)
        shapes = (
            jax.ShapeDtypeStruct((size, cols), F32),
            jax.ShapeDtypeStruct((size, cols), F32),
            jax.ShapeDtypeStruct((stacked, cols), F32),
        )
        operands = (
            tile[0], top[0], vectors[0], factor[0], rows[0, 0], pvectors[0], pfactor[0], parent, count[0, 0],
        )
        outs = pl.pallas_call(
            functools.partial(kernel, n_front, n_row),
            out_shape=shapes,
            in_specs=[hbm] * 9,
            out_specs=(vmem, vmem, vmem),
            scratch_shapes=[
                pltpu.VMEM((size, cols), F32),
                pltpu.VMEM((size, size), F32),
                pltpu.VMEM((size, size), F32),
                pltpu.VMEM(rows.shape[2:], jnp.int32),
                pltpu.VMEM((stacked, size), F32),
                pltpu.VMEM((size, size), F32),
                pltpu.SMEM(parent.shape, jnp.int32),
                pltpu.SMEM(count.shape[2:], jnp.int32),
                pltpu.SemaphoreType.DMA((8,)),
                pltpu.SemaphoreType.DMA((chunks,)),
                pltpu.VMEM((size, 3 * size), BF16),
                pltpu.VMEM((size, size), BF16),
                pltpu.VMEM((size, size), BF16),
                pltpu.VMEM((size, 3 * size), BF16),
                pltpu.VMEM((stacked, 3 * size), BF16),
                pltpu.VMEM((stacked, size), BF16),
                pltpu.VMEM((stacked, cols), F32),
                pltpu.VMEM((size, cols), F32),
                pltpu.VMEM((3 * size, cols), BF16),
                pltpu.VMEM((stacked, 3 * stacked), BF16),
                pltpu.VMEM((chunks, size, CHUNK), F32),
                pltpu.VMEM((chunks, n_front, cap, CHUNK), F32),
                pltpu.VMEM((chunks, n_front, cap, CHUNK), F32),
                pltpu.SemaphoreType.DMA((chunks, PIECES)),
                pltpu.SemaphoreType.DMA((chunks, PIECES)),
                pltpu.SemaphoreType.DMA((chunks, n_front)),
                pltpu.SemaphoreType.DMA((chunks, n_front)),
            ]
            + [pltpu.SemaphoreType.REGULAR] * 2,
            compiler_params=pltpu.CompilerParams(
                collective_id=0, has_side_effects=True, vmem_limit_bytes=40 * 1024 * 1024
            ),
        )(*[pltpu.with_memory_space_constraint(operand, pltpu.HBM) for operand in operands])
        outs = pl.pallas_call(
            write_out,
            out_shape=shapes,
            in_specs=[vmem] * 3,
            out_specs=(hbm, hbm, hbm),
            scratch_shapes=[pltpu.SemaphoreType.DMA((3,))],
        )(*[pltpu.with_memory_space_constraint(o, pltpu.VMEM) for o in outs])
        return tuple(out[None] for out in outs)

    placed = (
        P("front", "row", "col"),
        P("front", None, "col"),
        P("front", "row", None),
        P("front", "row", None),
        P(),
        P("front", "row", None, None),
        P("front", "row", None),
        P("front", "row", None),
        P("front", "row", None),
    )
    out = P("front", "row", "col")
    return jax.shard_map(
        shards, mesh=mesh, in_specs=placed, out_specs=(out, out, out), check_vma=False
    )
```

```python
import functools

import jax
import jax.numpy as jnp
from jax import lax
from jax.experimental import pallas as pl
from jax.experimental.pallas import tpu as pltpu
from jax.sharding import PartitionSpec as P

MESH = pl.DeviceIdType.MESH
F32, BF16 = jnp.float32, jnp.bfloat16
GROUPS = ((0, 128, 8), (128, 128, 8), (256, 128, 8), (384, 128, 8))
PARTS = ((0, 128, 0), (128, 128, 1), (256, 256, 3))
EARLY = 3


def split(x):
    high = x.astype(BF16)
    return high, (x - high.astype(F32)).astype(BF16)


def dot(left, right):
    return jnp.dot(left, right, preferred_element_type=F32)


def by_rows(left, right):
    lh, ll = split(left)
    rh, rl = split(right)
    return lax.dot_general(
        jnp.concatenate([lh, lh, ll], axis=1),
        jnp.concatenate([rh, rl, rh], axis=1),
        (((1,), (1,)), ((), ())),
        preferred_element_type=F32,
    )


def left_triple(x):
    high, low = split(x)
    return jnp.concatenate([high, high, low], axis=1)


def right_triple(x):
    high, low = split(x)
    return jnp.concatenate([high, low, high], axis=0)


def kernel(
    n_front,
    n_row,
    tile_in,
    top_in,
    vectors_in,
    factor_in,
    rows_in,
    pvectors_in,
    pfactor_in,
    parent_in,
    count_in,
    renewed,
    after,
    assembled,
    tile,
    vectors,
    factor,
    rows_ref,
    pvectors,
    pfactor,
    parent,
    count,
    loaded,
    top_loaded,
    vt3,
    tth,
    ttl,
    vf3,
    gvf3,
    picks,
    ga,
    proj,
    u3,
    h3,
    top_rx,
    z_tx,
    z_rx,
    chain_send,
    chain_recv,
    z_send,
    z_recv,
    fronts,
    everyone,
):
    front, row = lax.axis_index("front"), lax.axis_index("row")
    size, cols = tile.shape
    groups = range(len(GROUPS))
    spread, cap = rows_ref.shape
    slots = n_front * cap

    def columns(c):
        return pl.ds(GROUPS[c][0], GROUPS[c][1])

    def part_columns(c):
        return pl.ds(PARTS[c][0], PARTS[c][1])

    def top_load(c):
        return pltpu.make_async_copy(top_in.at[:, columns(c)], top_rx.at[:, columns(c)], top_loaded.at[c])

    pairs = (
        (vectors_in, vectors),
        (tile_in, tile),
        (factor_in, factor),
        (rows_in, rows_ref),
        (parent_in, parent),
        (count_in, count),
        (pvectors_in, pvectors),
        (pfactor_in, pfactor),
    )
    loads = [pltpu.make_async_copy(a, b, loaded.at[i]) for i, (a, b) in enumerate(pairs)]
    for load in loads[:3]:
        load.start()

    @pl.when(row == 0)
    def _():
        for c in groups:
            top_load(c).start()

    for load in loads[3:]:
        load.start()

    barrier = pltpu.get_barrier_semaphore()
    last = n_row - 1

    def tell(sem, **device):
        pl.semaphore_signal(sem, inc=1, device_id=device, device_id_type=MESH)

    def tell_fronts(sem):
        def one(step, carry):
            tell(sem, front=lax.rem(front + step, n_front))
            return carry

        lax.fori_loop(1, n_front, one, 0)

    @pl.when(row > 0)
    def _():
        tell(barrier, row=row - 1)

    @pl.when(row < last)
    def _():
        tell(barrier, row=last)

    @pl.when(row == last)
    def _():
        tell_fronts(barrier)

    def chain_copy(c, q):
        piece = size // GROUPS[c][2]
        part = pl.ds(q * piece, piece)
        return pltpu.make_async_remote_copy(
            src_ref=after.at[part, columns(c)],
            dst_ref=top_rx.at[part, columns(c)],
            send_sem=chain_send.at[c, q],
            recv_sem=chain_recv.at[c, q],
            device_id={"row": lax.rem(row + 1, n_row)},
            device_id_type=MESH,
        )

    def chain(c):
        piece = size // GROUPS[c][2]
        for q in range(GROUPS[c][2]):
            part = pl.ds(q * piece, piece)
            depth = min(size, -(-(q + 1) * piece // 128) * 128)

            @pl.when(row > 0)
            def _():
                chain_copy(c, q).wait_recv()

            entering = top_rx[part, columns(c)]
            high, low = split(entering + proj[part, columns(c)])
            u3[part, columns(c)] = high
            u3[pl.ds(size + q * piece, piece), columns(c)] = low
            u3[pl.ds(2 * size + q * piece, piece), columns(c)] = high
            first = u3[:depth, columns(c)]
            update = (
                dot(tth[part, :depth], first)
                + dot(tth[part, :depth], u3[size : size + depth, columns(c)])
                + dot(ttl[part, :depth], first)
            )
            after[part, columns(c)] = entering - update

            @pl.when(row < n_row - 1)
            def _():
                chain_copy(c, q).start()

    def z_copy(c, target, source):
        return pltpu.make_async_remote_copy(
            src_ref=z_tx.at[target, :, part_columns(c)],
            dst_ref=z_rx.at[source, :, part_columns(c)],
            send_sem=z_send.at[c, target],
            recv_sem=z_recv.at[c, source],
            device_id={"front": target},
            device_id_type=MESH,
        )

    def contribute(c):
        mine = part_columns(c)
        outgoing = ga[:, mine] - dot(gvf3[...], u3[:, mine])
        z_tx[:, :, mine] = outgoing.reshape(n_front, cap, PARTS[c][1])

        def send(step, carry):
            z_copy(c, lax.rem(front + step, n_front), front).start()
            return carry

        lax.fori_loop(1, n_front, send, 0)
        z_rx[front, :, mine] = z_tx[front, :, mine]

    @pl.when(row == last)
    def _():
        pl.semaphore_wait(barrier, n_front - 1 + last)
        tell_fronts(fronts)
        pl.semaphore_wait(fronts, n_front - 1)
        for r in range(last):
            tell(everyone, row=r)

    loads[0].wait()
    vt3[...] = left_triple(vectors[...].T)
    loads[2].wait()
    high, low = split(factor[...].T)
    tth[...], ttl[...] = high, low
    loads[1].wait()

    def project(mine):
        proj[:, mine] = dot(vt3[...], right_triple(tile[:, mine]))
        u3[:, mine] = jnp.zeros((3 * size, mine.size), BF16)

    project(columns(0))

    @pl.when(row < last)
    def _():
        pl.semaphore_wait(barrier, 1)

    @pl.when(row == 0)
    def _():
        for c in groups:
            top_load(c).wait()
        chain(0)

    project(pl.ds(GROUPS[0][1], cols - GROUPS[0][1]))
    for load in loads[3:]:
        load.wait()

    first = lax.rem(parent[front], n_front)
    lane = lax.broadcasted_iota(jnp.int32, (1, cap), 1)
    listed = []
    for g in range(n_front):
        k = lax.rem(g + n_front - first, n_front)
        held = jnp.minimum(k, spread - 1)
        sent = jnp.where(k < spread, count[held], 0)
        listed.append(jnp.where(lane < sent, rows_ref[pl.ds(held, 1), :], -1))
    wanted = jnp.concatenate(listed, axis=1)
    chosen = lax.broadcasted_iota(jnp.int32, (size, slots), 0) == wanted
    picks[...] = jnp.where(chosen, 1.0, 0.0).T.astype(BF16)

    vh, vl = split(by_rows(vectors[...], factor[...]))
    vf3[...] = jnp.concatenate([vh, vh, vl], axis=1)
    gvh = dot(picks[...], vh).astype(BF16)
    gvf3[...] = jnp.concatenate([gvh, gvh, dot(picks[...], vl).astype(BF16)], axis=1)
    th, tl = split(tile[...])
    ga[...] = dot(picks[...], th) + dot(picks[...], tl)

    for c in groups:
        if c == 0:

            @pl.when(row > 0)
            def _():
                chain(c)

            @pl.when(jnp.logical_and(row >= EARLY, row < last))
            def _():
                pl.semaphore_wait(everyone, 1)

        else:
            chain(c)

        for i, (_, _, needed) in enumerate(PARTS):
            if needed == c:

                @pl.when(row >= EARLY)
                def _():
                    contribute(i)

    @pl.when(row < EARLY)
    def _():
        pl.semaphore_wait(everyone, 1)
        for i in range(len(PARTS)):
            contribute(i)

    renewed[...] = tile[...] - dot(vf3[...], u3[...])
    h3[...] = left_triple(by_rows(by_rows(pvectors[...], pfactor[...]), pvectors[...]))

    @pl.when(row < last)
    def _():
        for c in groups:
            for q in range(GROUPS[c][2]):
                chain_copy(c, q).wait_send()

    for i, (start, width, _) in enumerate(PARTS):

        def left(step, inner):
            z_copy(i, lax.rem(front + step, n_front), front).wait_send()
            return inner

        def arrive(step, inner):
            z_copy(i, front, lax.rem(front + step, n_front)).wait_recv()
            return inner

        lax.fori_loop(1, n_front, left, 0)
        lax.fori_loop(1, n_front, arrive, 0)
        stacked = z_rx[:, :, start : start + width].reshape(slots, width)
        assembled[:, start : start + width] = stacked - dot(h3[...], right_triple(stacked))


def write_out(*refs):
    results, arrays, sems = refs[:3], refs[3:6], refs[6]
    copies = [
        pltpu.make_async_copy(result, array, sems.at[i])
        for i, (result, array) in enumerate(zip(results, arrays))
    ]
    for copy in copies:
        copy.start()
    for copy in copies:
        copy.wait()


def solution(mesh):
    n_front, n_row = mesh.shape["front"], mesh.shape["row"]

    def shards(tile, top, vectors, factor, parent, rows, count, pvectors, pfactor):
        size, cols = tile.shape[1:]
        stacked = pvectors.shape[1]
        cap = rows.shape[3]
        groups = len(GROUPS)
        pieces = max(pieces for _, _, pieces in GROUPS)
        vmem = pl.BlockSpec(memory_space=pltpu.VMEM)
        hbm = pl.BlockSpec(memory_space=pltpu.HBM)
        shapes = (
            jax.ShapeDtypeStruct((size, cols), F32),
            jax.ShapeDtypeStruct((size, cols), F32),
            jax.ShapeDtypeStruct((stacked, cols), F32),
        )
        operands = (
            tile[0], top[0], vectors[0], factor[0], rows[0, 0], pvectors[0], pfactor[0], parent, count[0, 0],
        )
        outs = pl.pallas_call(
            functools.partial(kernel, n_front, n_row),
            out_shape=shapes,
            in_specs=[hbm] * 9,
            out_specs=(vmem, vmem, vmem),
            scratch_shapes=[
                pltpu.VMEM((size, cols), F32),
                pltpu.VMEM((size, size), F32),
                pltpu.VMEM((size, size), F32),
                pltpu.VMEM(rows.shape[2:], jnp.int32),
                pltpu.VMEM((stacked, size), F32),
                pltpu.VMEM((size, size), F32),
                pltpu.SMEM(parent.shape, jnp.int32),
                pltpu.SMEM(count.shape[2:], jnp.int32),
                pltpu.SemaphoreType.DMA((8,)),
                pltpu.SemaphoreType.DMA((groups,)),
                pltpu.VMEM((size, 3 * size), BF16),
                pltpu.VMEM((size, size), BF16),
                pltpu.VMEM((size, size), BF16),
                pltpu.VMEM((size, 3 * size), BF16),
                pltpu.VMEM((stacked, 3 * size), BF16),
                pltpu.VMEM((stacked, size), BF16),
                pltpu.VMEM((stacked, cols), F32),
                pltpu.VMEM((size, cols), F32),
                pltpu.VMEM((3 * size, cols), BF16),
                pltpu.VMEM((stacked, 3 * stacked), BF16),
                pltpu.VMEM((size, cols), F32),
                pltpu.VMEM((n_front, cap, cols), F32),
                pltpu.VMEM((n_front, cap, cols), F32),
                pltpu.SemaphoreType.DMA((groups, pieces)),
                pltpu.SemaphoreType.DMA((groups, pieces)),
                pltpu.SemaphoreType.DMA((len(PARTS), n_front)),
                pltpu.SemaphoreType.DMA((len(PARTS), n_front)),
            ]
            + [pltpu.SemaphoreType.REGULAR] * 2,
            compiler_params=pltpu.CompilerParams(
                collective_id=0, has_side_effects=True, vmem_limit_bytes=40 * 1024 * 1024
            ),
        )(*[pltpu.with_memory_space_constraint(operand, pltpu.HBM) for operand in operands])
        outs = pl.pallas_call(
            write_out,
            out_shape=shapes,
            in_specs=[vmem] * 3,
            out_specs=(hbm, hbm, hbm),
            scratch_shapes=[pltpu.SemaphoreType.DMA((3,))],
        )(*[pltpu.with_memory_space_constraint(o, pltpu.VMEM) for o in outs])
        return tuple(out[None] for out in outs)

    placed = (
        P("front", "row", "col"),
        P("front", None, "col"),
        P("front", "row", None),
        P("front", "row", None),
        P(),
        P("front", "row", None, None),
        P("front", "row", None),
        P("front", "row", None),
        P("front", "row", None),
    )
    out = P("front", "row", "col")
    return jax.shard_map(
        shards, mesh=mesh, in_specs=placed, out_specs=(out, out, out), check_vma=False
    )
```

```python
import functools

import jax
import jax.numpy as jnp
from jax import lax
from jax.experimental import pallas as pl
from jax.experimental.pallas import tpu as pltpu
from jax.sharding import PartitionSpec as P

MESH = pl.DeviceIdType.MESH
F32, BF16 = jnp.float32, jnp.bfloat16
GROUPS = ((0, 128, 8), (128, 128, 8), (256, 128, 8), (384, 128, 8))
PARTS = ((0, 128, 0), (128, 128, 1), (256, 256, 3))
EARLY = 5


def split(x):
    high = x.astype(BF16)
    return high, (x - high.astype(F32)).astype(BF16)


def dot(left, right):
    return jnp.dot(left, right, preferred_element_type=F32)


def by_rows(left, right):
    lh, ll = split(left)
    rh, rl = split(right)
    return lax.dot_general(
        jnp.concatenate([lh, lh, ll], axis=1),
        jnp.concatenate([rh, rl, rh], axis=1),
        (((1,), (1,)), ((), ())),
        preferred_element_type=F32,
    )


def left_triple(x):
    high, low = split(x)
    return jnp.concatenate([high, high, low], axis=1)


def right_triple(x):
    high, low = split(x)
    return jnp.concatenate([high, low, high], axis=0)


def kernel(
    n_front,
    n_row,
    tile_in,
    top_in,
    vectors_in,
    factor_in,
    rows_in,
    pvectors_in,
    pfactor_in,
    parent_in,
    count_in,
    renewed,
    after,
    assembled,
    tile,
    vectors,
    factor,
    rows_ref,
    pvectors,
    pfactor,
    parent,
    count,
    loaded,
    top_loaded,
    vt3,
    tth,
    ttl,
    vf3,
    gvf3,
    picks,
    ga,
    proj,
    u3,
    h3,
    top_rx,
    z_tx,
    z_rx,
    chain_send,
    chain_recv,
    z_send,
    z_recv,
    fronts,
    everyone,
):
    front, row = lax.axis_index("front"), lax.axis_index("row")
    size, cols = tile.shape
    groups = range(len(GROUPS))
    spread, cap = rows_ref.shape
    slots = n_front * cap

    def columns(c):
        return pl.ds(GROUPS[c][0], GROUPS[c][1])

    def part_columns(c):
        return pl.ds(PARTS[c][0], PARTS[c][1])

    def top_load(c):
        return pltpu.make_async_copy(top_in.at[:, columns(c)], top_rx.at[:, columns(c)], top_loaded.at[c])

    pairs = (
        (vectors_in, vectors),
        (tile_in, tile),
        (factor_in, factor),
        (rows_in, rows_ref),
        (parent_in, parent),
        (count_in, count),
        (pvectors_in, pvectors),
        (pfactor_in, pfactor),
    )
    loads = [pltpu.make_async_copy(a, b, loaded.at[i]) for i, (a, b) in enumerate(pairs)]
    for load in loads[:3]:
        load.start()

    @pl.when(row == 0)
    def _():
        for c in groups:
            top_load(c).start()

    for load in loads[3:]:
        load.start()

    barrier = pltpu.get_barrier_semaphore()
    last = n_row - 1

    def tell(sem, **device):
        pl.semaphore_signal(sem, inc=1, device_id=device, device_id_type=MESH)

    def tell_fronts(sem):
        def one(step, carry):
            tell(sem, front=lax.rem(front + step, n_front))
            return carry

        lax.fori_loop(1, n_front, one, 0)

    @pl.when(row > 0)
    def _():
        tell(barrier, row=row - 1)

    @pl.when(row < last)
    def _():
        tell(barrier, row=last)

    @pl.when(row == last)
    def _():
        tell_fronts(barrier)

    def chain_copy(c, q):
        piece = size // GROUPS[c][2]
        part = pl.ds(q * piece, piece)
        return pltpu.make_async_remote_copy(
            src_ref=after.at[part, columns(c)],
            dst_ref=top_rx.at[part, columns(c)],
            send_sem=chain_send.at[c, q],
            recv_sem=chain_recv.at[c, q],
            device_id={"row": lax.rem(row + 1, n_row)},
            device_id_type=MESH,
        )

    def chain(c):
        piece = size // GROUPS[c][2]
        for q in range(GROUPS[c][2]):
            part = pl.ds(q * piece, piece)
            depth = min(size, -(-(q + 1) * piece // 128) * 128)

            @pl.when(row > 0)
            def _():
                chain_copy(c, q).wait_recv()

            entering = top_rx[part, columns(c)]
            high, low = split(entering + proj[part, columns(c)])
            u3[part, columns(c)] = high
            u3[pl.ds(size + q * piece, piece), columns(c)] = low
            u3[pl.ds(2 * size + q * piece, piece), columns(c)] = high
            first = u3[:depth, columns(c)]
            update = (
                dot(tth[part, :depth], first)
                + dot(tth[part, :depth], u3[size : size + depth, columns(c)])
                + dot(ttl[part, :depth], first)
            )
            after[part, columns(c)] = entering - update

            @pl.when(row < n_row - 1)
            def _():
                chain_copy(c, q).start()

    def z_copy(c, target, source):
        return pltpu.make_async_remote_copy(
            src_ref=z_tx.at[target, :, part_columns(c)],
            dst_ref=z_rx.at[source, :, part_columns(c)],
            send_sem=z_send.at[c, target],
            recv_sem=z_recv.at[c, source],
            device_id={"front": target},
            device_id_type=MESH,
        )

    def contribute(c):
        mine = part_columns(c)
        outgoing = ga[:, mine] - dot(gvf3[...], u3[:, mine])
        z_tx[:, :, mine] = outgoing.reshape(n_front, cap, PARTS[c][1])

        def across(step, carry):
            z_copy(c, (1 - half) * (n_front // 2) + lax.rem(place + step, n_front // 2), front).start()
            return carry

        def along(step, carry):
            z_copy(c, half * (n_front // 2) + lax.rem(place + step, n_front // 2), front).start()
            return carry

        half, place = lax.div(front, n_front // 2), lax.rem(front, n_front // 2)
        lax.fori_loop(0, n_front // 2, across, 0)
        lax.fori_loop(1, n_front // 2, along, 0)
        z_rx[front, :, mine] = z_tx[front, :, mine]

    @pl.when(row == last)
    def _():
        pl.semaphore_wait(barrier, n_front - 1 + last)
        tell_fronts(fronts)
        pl.semaphore_wait(fronts, n_front - 1)
        for r in range(last):
            tell(everyone, row=r)

    loads[0].wait()
    vt3[...] = left_triple(vectors[...].T)
    loads[2].wait()
    high, low = split(factor[...].T)
    tth[...], ttl[...] = high, low
    loads[1].wait()

    def project(mine):
        proj[:, mine] = dot(vt3[...], right_triple(tile[:, mine]))
        u3[:, mine] = jnp.zeros((3 * size, mine.size), BF16)

    project(columns(0))

    @pl.when(row < last)
    def _():
        pl.semaphore_wait(barrier, 1)

    @pl.when(row == 0)
    def _():
        for c in groups:
            top_load(c).wait()
        chain(0)

    project(pl.ds(GROUPS[0][1], cols - GROUPS[0][1]))
    for load in loads[3:]:
        load.wait()

    first = lax.rem(parent[front], n_front)
    lane = lax.broadcasted_iota(jnp.int32, (1, cap), 1)
    listed = []
    for g in range(n_front):
        k = lax.rem(g + n_front - first, n_front)
        held = jnp.minimum(k, spread - 1)
        sent = jnp.where(k < spread, count[held], 0)
        listed.append(jnp.where(lane < sent, rows_ref[pl.ds(held, 1), :], -1))
    wanted = jnp.concatenate(listed, axis=1)
    chosen = lax.broadcasted_iota(jnp.int32, (size, slots), 0) == wanted
    picks[...] = jnp.where(chosen, 1.0, 0.0).T.astype(BF16)

    vh, vl = split(by_rows(vectors[...], factor[...]))
    vf3[...] = jnp.concatenate([vh, vh, vl], axis=1)
    gvh = dot(picks[...], vh).astype(BF16)
    gvf3[...] = jnp.concatenate([gvh, gvh, dot(picks[...], vl).astype(BF16)], axis=1)
    th, tl = split(tile[...])
    ga[...] = dot(picks[...], th) + dot(picks[...], tl)

    for c in groups:
        if c == 0:

            @pl.when(row > 0)
            def _():
                chain(c)

            @pl.when(jnp.logical_and(row >= EARLY, row < last))
            def _():
                pl.semaphore_wait(everyone, 1)

        else:
            chain(c)

        for i, (_, _, needed) in enumerate(PARTS):
            if needed == c:

                @pl.when(row >= EARLY)
                def _():
                    contribute(i)

    @pl.when(row < EARLY)
    def _():
        pl.semaphore_wait(everyone, 1)
        for i in range(len(PARTS)):
            contribute(i)

    renewed[...] = tile[...] - dot(vf3[...], u3[...])
    h3[...] = left_triple(by_rows(by_rows(pvectors[...], pfactor[...]), pvectors[...]))

    @pl.when(row < last)
    def _():
        for c in groups:
            for q in range(GROUPS[c][2]):
                chain_copy(c, q).wait_send()

    for i, (start, width, _) in enumerate(PARTS):

        def left(step, inner):
            z_copy(i, lax.rem(front + step, n_front), front).wait_send()
            return inner

        def arrive(step, inner):
            z_copy(i, front, lax.rem(front + step, n_front)).wait_recv()
            return inner

        lax.fori_loop(1, n_front, left, 0)
        lax.fori_loop(1, n_front, arrive, 0)
        stacked = z_rx[:, :, start : start + width].reshape(slots, width)
        assembled[:, start : start + width] = stacked - dot(h3[...], right_triple(stacked))


def write_out(*refs):
    results, arrays, sems = refs[:3], refs[3:6], refs[6]
    copies = [
        pltpu.make_async_copy(result, array, sems.at[i])
        for i, (result, array) in enumerate(zip(results, arrays))
    ]
    for copy in copies:
        copy.start()
    for copy in copies:
        copy.wait()


def solution(mesh):
    n_front, n_row = mesh.shape["front"], mesh.shape["row"]

    def shards(tile, top, vectors, factor, parent, rows, count, pvectors, pfactor):
        size, cols = tile.shape[1:]
        stacked = pvectors.shape[1]
        cap = rows.shape[3]
        groups = len(GROUPS)
        pieces = max(pieces for _, _, pieces in GROUPS)
        vmem = pl.BlockSpec(memory_space=pltpu.VMEM)
        hbm = pl.BlockSpec(memory_space=pltpu.HBM)
        shapes = (
            jax.ShapeDtypeStruct((size, cols), F32),
            jax.ShapeDtypeStruct((size, cols), F32),
            jax.ShapeDtypeStruct((stacked, cols), F32),
        )
        operands = (
            tile[0], top[0], vectors[0], factor[0], rows[0, 0], pvectors[0], pfactor[0], parent, count[0, 0],
        )
        outs = pl.pallas_call(
            functools.partial(kernel, n_front, n_row),
            out_shape=shapes,
            in_specs=[hbm] * 9,
            out_specs=(vmem, vmem, vmem),
            scratch_shapes=[
                pltpu.VMEM((size, cols), F32),
                pltpu.VMEM((size, size), F32),
                pltpu.VMEM((size, size), F32),
                pltpu.VMEM(rows.shape[2:], jnp.int32),
                pltpu.VMEM((stacked, size), F32),
                pltpu.VMEM((size, size), F32),
                pltpu.SMEM(parent.shape, jnp.int32),
                pltpu.SMEM(count.shape[2:], jnp.int32),
                pltpu.SemaphoreType.DMA((8,)),
                pltpu.SemaphoreType.DMA((groups,)),
                pltpu.VMEM((size, 3 * size), BF16),
                pltpu.VMEM((size, size), BF16),
                pltpu.VMEM((size, size), BF16),
                pltpu.VMEM((size, 3 * size), BF16),
                pltpu.VMEM((stacked, 3 * size), BF16),
                pltpu.VMEM((stacked, size), BF16),
                pltpu.VMEM((stacked, cols), F32),
                pltpu.VMEM((size, cols), F32),
                pltpu.VMEM((3 * size, cols), BF16),
                pltpu.VMEM((stacked, 3 * stacked), BF16),
                pltpu.VMEM((size, cols), F32),
                pltpu.VMEM((n_front, cap, cols), F32),
                pltpu.VMEM((n_front, cap, cols), F32),
                pltpu.SemaphoreType.DMA((groups, pieces)),
                pltpu.SemaphoreType.DMA((groups, pieces)),
                pltpu.SemaphoreType.DMA((len(PARTS), n_front)),
                pltpu.SemaphoreType.DMA((len(PARTS), n_front)),
            ]
            + [pltpu.SemaphoreType.REGULAR] * 2,
            compiler_params=pltpu.CompilerParams(
                collective_id=0, has_side_effects=True, vmem_limit_bytes=40 * 1024 * 1024
            ),
        )(*[pltpu.with_memory_space_constraint(operand, pltpu.HBM) for operand in operands])
        outs = pl.pallas_call(
            write_out,
            out_shape=shapes,
            in_specs=[vmem] * 3,
            out_specs=(hbm, hbm, hbm),
            scratch_shapes=[pltpu.SemaphoreType.DMA((3,))],
        )(*[pltpu.with_memory_space_constraint(o, pltpu.VMEM) for o in outs])
        return tuple(out[None] for out in outs)

    placed = (
        P("front", "row", "col"),
        P("front", None, "col"),
        P("front", "row", None),
        P("front", "row", None),
        P(),
        P("front", "row", None, None),
        P("front", "row", None),
        P("front", "row", None),
        P("front", "row", None),
    )
    out = P("front", "row", "col")
    return jax.shard_map(
        shards, mesh=mesh, in_specs=placed, out_specs=(out, out, out), check_vma=False
    )
```

```python
import functools

import jax
import jax.numpy as jnp
from jax import lax
from jax.experimental import pallas as pl
from jax.experimental.pallas import tpu as pltpu
from jax.sharding import PartitionSpec as P

MESH = pl.DeviceIdType.MESH
F32, BF16 = jnp.float32, jnp.bfloat16
GROUPS = ((0, 128, 8), (128, 128, 8), (256, 128, 8), (384, 128, 8))
PARTS = ((0, 128, 0), (128, 128, 1), (256, 256, 3))
LAGS = (6, 4, 3)


def split(x):
    high = x.astype(BF16)
    return high, (x - high.astype(F32)).astype(BF16)


def dot(left, right):
    return jnp.dot(left, right, preferred_element_type=F32)


def by_rows(left, right):
    lh, ll = split(left)
    rh, rl = split(right)
    return lax.dot_general(
        jnp.concatenate([lh, lh, ll], axis=1),
        jnp.concatenate([rh, rl, rh], axis=1),
        (((1,), (1,)), ((), ())),
        preferred_element_type=F32,
    )


def left_triple(x):
    high, low = split(x)
    return jnp.concatenate([high, high, low], axis=1)


def right_triple(x):
    high, low = split(x)
    return jnp.concatenate([high, low, high], axis=0)


def kernel(
    n_front,
    n_row,
    tile_in,
    top_in,
    vectors_in,
    factor_in,
    rows_in,
    pvectors_in,
    pfactor_in,
    parent_in,
    count_in,
    renewed,
    after,
    assembled,
    tile,
    vectors,
    factor,
    rows_ref,
    pvectors,
    pfactor,
    parent,
    count,
    loaded,
    top_loaded,
    vt3,
    tth,
    ttl,
    vf3,
    gvf3,
    picks,
    ga,
    proj,
    u3,
    h3,
    top_rx,
    z_tx,
    z_rx,
    chain_send,
    chain_recv,
    z_send,
    z_recv,
    fronts,
    everyone,
):
    front, row = lax.axis_index("front"), lax.axis_index("row")
    size, cols = tile.shape
    groups = range(len(GROUPS))
    spread, cap = rows_ref.shape
    slots = n_front * cap

    def columns(c):
        return pl.ds(GROUPS[c][0], GROUPS[c][1])

    def part_columns(c):
        return pl.ds(PARTS[c][0], PARTS[c][1])

    def top_load(c):
        return pltpu.make_async_copy(top_in.at[:, columns(c)], top_rx.at[:, columns(c)], top_loaded.at[c])

    pairs = (
        (vectors_in, vectors),
        (tile_in, tile),
        (factor_in, factor),
        (rows_in, rows_ref),
        (parent_in, parent),
        (count_in, count),
        (pvectors_in, pvectors),
        (pfactor_in, pfactor),
    )
    loads = [pltpu.make_async_copy(a, b, loaded.at[i]) for i, (a, b) in enumerate(pairs)]
    for load in loads[:3]:
        load.start()

    @pl.when(row == 0)
    def _():
        for c in groups:
            top_load(c).start()

    for load in loads[3:]:
        load.start()

    barrier = pltpu.get_barrier_semaphore()
    last = n_row - 1

    def tell(sem, **device):
        pl.semaphore_signal(sem, inc=1, device_id=device, device_id_type=MESH)

    def tell_fronts(sem):
        def one(step, carry):
            tell(sem, front=lax.rem(front + step, n_front))
            return carry

        lax.fori_loop(1, n_front, one, 0)

    @pl.when(row > 0)
    def _():
        tell(barrier, row=row - 1)

    @pl.when(row < last)
    def _():
        tell(barrier, row=last)

    @pl.when(row == last)
    def _():
        tell_fronts(barrier)

    def chain_copy(c, q):
        piece = size // GROUPS[c][2]
        part = pl.ds(q * piece, piece)
        return pltpu.make_async_remote_copy(
            src_ref=after.at[part, columns(c)],
            dst_ref=top_rx.at[part, columns(c)],
            send_sem=chain_send.at[c, q],
            recv_sem=chain_recv.at[c, q],
            device_id={"row": lax.rem(row + 1, n_row)},
            device_id_type=MESH,
        )

    def chain(c):
        piece = size // GROUPS[c][2]
        for q in range(GROUPS[c][2]):
            part = pl.ds(q * piece, piece)
            depth = min(size, -(-(q + 1) * piece // 128) * 128)

            @pl.when(row > 0)
            def _():
                chain_copy(c, q).wait_recv()

            entering = top_rx[part, columns(c)]
            high, low = split(entering + proj[part, columns(c)])
            u3[part, columns(c)] = high
            u3[pl.ds(size + q * piece, piece), columns(c)] = low
            u3[pl.ds(2 * size + q * piece, piece), columns(c)] = high
            first = u3[:depth, columns(c)]
            update = (
                dot(tth[part, :depth], first)
                + dot(tth[part, :depth], u3[size : size + depth, columns(c)])
                + dot(ttl[part, :depth], first)
            )
            after[part, columns(c)] = entering - update

            @pl.when(row < n_row - 1)
            def _():
                chain_copy(c, q).start()

    def z_copy(c, target, source):
        return pltpu.make_async_remote_copy(
            src_ref=z_tx.at[target, :, part_columns(c)],
            dst_ref=z_rx.at[source, :, part_columns(c)],
            send_sem=z_send.at[c, target],
            recv_sem=z_recv.at[c, source],
            device_id={"front": target},
            device_id_type=MESH,
        )

    def contribute(c):
        mine = part_columns(c)
        outgoing = ga[:, mine] - dot(gvf3[...], u3[:, mine])
        z_tx[:, :, mine] = outgoing.reshape(n_front, cap, PARTS[c][1])

        def across(step, carry):
            z_copy(c, (1 - half) * (n_front // 2) + lax.rem(place + step, n_front // 2), front).start()
            return carry

        def along(step, carry):
            z_copy(c, half * (n_front // 2) + lax.rem(place + step, n_front // 2), front).start()
            return carry

        half, place = lax.div(front, n_front // 2), lax.rem(front, n_front // 2)
        lax.fori_loop(0, n_front // 2, across, 0)
        lax.fori_loop(1, n_front // 2, along, 0)
        z_rx[front, :, mine] = z_tx[front, :, mine]

    @pl.when(row == last)
    def _():
        pl.semaphore_wait(barrier, n_front - 1 + last)
        tell_fronts(fronts)
        pl.semaphore_wait(fronts, n_front - 1)
        for r in range(last):
            tell(everyone, row=r)

    loads[0].wait()
    vt3[...] = left_triple(vectors[...].T)
    loads[2].wait()
    high, low = split(factor[...].T)
    tth[...], ttl[...] = high, low
    loads[1].wait()

    def project(mine):
        proj[:, mine] = dot(vt3[...], right_triple(tile[:, mine]))
        u3[:, mine] = jnp.zeros((3 * size, mine.size), BF16)

    project(columns(0))

    @pl.when(row < last)
    def _():
        pl.semaphore_wait(barrier, 1)

    @pl.when(row == 0)
    def _():
        for c in groups:
            top_load(c).wait()
        mine = columns(0)
        high, low = split(top_rx[:, mine] + proj[:, mine])
        u3[:size, mine], u3[size : 2 * size, mine], u3[2 * size :, mine] = high, low, high
        update = dot(tth[...], high) + dot(tth[...], low) + dot(ttl[...], high)
        after[:, mine] = top_rx[:, mine] - update
        for q in range(GROUPS[0][2]):
            chain_copy(0, q).start()

    project(pl.ds(GROUPS[0][1], cols - GROUPS[0][1]))
    for load in loads[3:]:
        load.wait()

    first = lax.rem(parent[front], n_front)
    lane = lax.broadcasted_iota(jnp.int32, (1, cap), 1)
    listed = []
    for g in range(n_front):
        k = lax.rem(g + n_front - first, n_front)
        held = jnp.minimum(k, spread - 1)
        sent = jnp.where(k < spread, count[held], 0)
        listed.append(jnp.where(lane < sent, rows_ref[pl.ds(held, 1), :], -1))
    wanted = jnp.concatenate(listed, axis=1)
    chosen = lax.broadcasted_iota(jnp.int32, (size, slots), 0) == wanted
    picks[...] = jnp.where(chosen, 1.0, 0.0).T.astype(BF16)

    vh, vl = split(by_rows(vectors[...], factor[...]))
    vf3[...] = jnp.concatenate([vh, vh, vl], axis=1)
    gvh = dot(picks[...], vh).astype(BF16)
    gvf3[...] = jnp.concatenate([gvh, gvh, dot(picks[...], vl).astype(BF16)], axis=1)
    th, tl = split(tile[...])
    ga[...] = dot(picks[...], th) + dot(picks[...], tl)

    lag = sum(jnp.where(row < bound, 1, 0) for bound in LAGS)
    for c in groups:
        if c == 0:

            @pl.when(row > 0)
            def _():
                chain(c)

            @pl.when(jnp.logical_and(lag == 0, row < last))
            def _():
                pl.semaphore_wait(everyone, 1)

        else:
            chain(c)

        if 0 < c < len(LAGS) + 1:

            @pl.when(lag == c)
            def _():
                pl.semaphore_wait(everyone, 1)

        for i, (_, _, needed) in enumerate(PARTS):
            if c >= needed:

                @pl.when(lag == c - needed)
                def _():
                    contribute(i)

    for i, (_, _, needed) in enumerate(PARTS):

        @pl.when(lag > len(GROUPS) - 1 - needed)
        def _():
            contribute(i)

    renewed[...] = tile[...] - dot(vf3[...], u3[...])
    h3[...] = left_triple(by_rows(by_rows(pvectors[...], pfactor[...]), pvectors[...]))

    @pl.when(row < last)
    def _():
        for c in groups:
            for q in range(GROUPS[c][2]):
                chain_copy(c, q).wait_send()

    for i, (start, width, _) in enumerate(PARTS):

        def left(step, inner):
            z_copy(i, lax.rem(front + step, n_front), front).wait_send()
            return inner

        def arrive(step, inner):
            z_copy(i, front, lax.rem(front + step, n_front)).wait_recv()
            return inner

        lax.fori_loop(1, n_front, left, 0)
        lax.fori_loop(1, n_front, arrive, 0)
        stacked = z_rx[:, :, start : start + width].reshape(slots, width)
        assembled[:, start : start + width] = stacked - dot(h3[...], right_triple(stacked))


def write_out(*refs):
    results, arrays, sems = refs[:3], refs[3:6], refs[6]
    copies = [
        pltpu.make_async_copy(result, array, sems.at[i])
        for i, (result, array) in enumerate(zip(results, arrays))
    ]
    for copy in copies:
        copy.start()
    for copy in copies:
        copy.wait()


def solution(mesh):
    n_front, n_row = mesh.shape["front"], mesh.shape["row"]

    def shards(tile, top, vectors, factor, parent, rows, count, pvectors, pfactor):
        size, cols = tile.shape[1:]
        stacked = pvectors.shape[1]
        cap = rows.shape[3]
        groups = len(GROUPS)
        pieces = max(pieces for _, _, pieces in GROUPS)
        vmem = pl.BlockSpec(memory_space=pltpu.VMEM)
        hbm = pl.BlockSpec(memory_space=pltpu.HBM)
        shapes = (
            jax.ShapeDtypeStruct((size, cols), F32),
            jax.ShapeDtypeStruct((size, cols), F32),
            jax.ShapeDtypeStruct((stacked, cols), F32),
        )
        operands = (
            tile[0], top[0], vectors[0], factor[0], rows[0, 0], pvectors[0], pfactor[0], parent, count[0, 0],
        )
        outs = pl.pallas_call(
            functools.partial(kernel, n_front, n_row),
            out_shape=shapes,
            in_specs=[hbm] * 9,
            out_specs=(vmem, vmem, vmem),
            scratch_shapes=[
                pltpu.VMEM((size, cols), F32),
                pltpu.VMEM((size, size), F32),
                pltpu.VMEM((size, size), F32),
                pltpu.VMEM(rows.shape[2:], jnp.int32),
                pltpu.VMEM((stacked, size), F32),
                pltpu.VMEM((size, size), F32),
                pltpu.SMEM(parent.shape, jnp.int32),
                pltpu.SMEM(count.shape[2:], jnp.int32),
                pltpu.SemaphoreType.DMA((8,)),
                pltpu.SemaphoreType.DMA((groups,)),
                pltpu.VMEM((size, 3 * size), BF16),
                pltpu.VMEM((size, size), BF16),
                pltpu.VMEM((size, size), BF16),
                pltpu.VMEM((size, 3 * size), BF16),
                pltpu.VMEM((stacked, 3 * size), BF16),
                pltpu.VMEM((stacked, size), BF16),
                pltpu.VMEM((stacked, cols), F32),
                pltpu.VMEM((size, cols), F32),
                pltpu.VMEM((3 * size, cols), BF16),
                pltpu.VMEM((stacked, 3 * stacked), BF16),
                pltpu.VMEM((size, cols), F32),
                pltpu.VMEM((n_front, cap, cols), F32),
                pltpu.VMEM((n_front, cap, cols), F32),
                pltpu.SemaphoreType.DMA((groups, pieces)),
                pltpu.SemaphoreType.DMA((groups, pieces)),
                pltpu.SemaphoreType.DMA((len(PARTS), n_front)),
                pltpu.SemaphoreType.DMA((len(PARTS), n_front)),
            ]
            + [pltpu.SemaphoreType.REGULAR] * 2,
            compiler_params=pltpu.CompilerParams(
                collective_id=0, has_side_effects=True, vmem_limit_bytes=40 * 1024 * 1024
            ),
        )(*[pltpu.with_memory_space_constraint(operand, pltpu.HBM) for operand in operands])
        outs = pl.pallas_call(
            write_out,
            out_shape=shapes,
            in_specs=[vmem] * 3,
            out_specs=(hbm, hbm, hbm),
            scratch_shapes=[pltpu.SemaphoreType.DMA((3,))],
        )(*[pltpu.with_memory_space_constraint(o, pltpu.VMEM) for o in outs])
        return tuple(out[None] for out in outs)

    placed = (
        P("front", "row", "col"),
        P("front", None, "col"),
        P("front", "row", None),
        P("front", "row", None),
        P(),
        P("front", "row", None, None),
        P("front", "row", None),
        P("front", "row", None),
        P("front", "row", None),
    )
    out = P("front", "row", "col")
    return jax.shard_map(
        shards, mesh=mesh, in_specs=placed, out_specs=(out, out, out), check_vma=False
    )
```
